32 devices in a mesh: seq: 16 (over z, y, x), ch: 2 (over core).
Axes of the slice: x: 2, y: 2, z: 4, core: 2. Of those that a mesh axis runs over, the one named last changes fastest.
Arguments:
- gate_outer: bfloat16 [2048, 4096], P('seq', 'ch'), may hold values from -6 to 6
- gate_inner: bfloat16 [2048, 4096], P('seq', 'ch'), may hold values from -6 to 6
- values_in: bfloat16 [2048, 4096], P('seq', 'ch'), may hold values from -6 to 6
- filter_taps: bfloat16 [2048, 512], P('seq', 'ch'), may hold values from -2.5 to 2.5
- skip_gain: float32 [4096], P('ch'), may hold values from -4 to 4
Outputs:
- mixed_output: bfloat16 [2048, 4096], P('seq', 'ch')
The draws below stay inside these ranges and needn't reach their ends.
All inputs are finite; a program needn't handle non-finite values.
Results may differ from the reference program's by a relative error of at most 0.0065.
Values may be sent and summed in bfloat16 or wider, within the bound.
A program may use at most 64 MiB of HBM per device.

```python
import jax
import jax.numpy as jnp
from jax import lax

C = 4096
G = 512
SEQ_LEN = 2048


def energy_total(span_lengths):
    return (1.0 - jnp.exp(-2.0 * SEQ_LEN / span_lengths)) / (1.0 - jnp.exp(-2.0 / span_lengths))


def draw_filter_taps(key, part):
    key = jax.random.fold_in(key, 11)
    head_key, tail_key, share_key, tap_key = jax.random.split(key, 4)
    head_spans = jnp.exp(jax.random.uniform(head_key, (G,), jnp.float32, jnp.log(8.0), jnp.log(256.0)))
    tail_spans = jnp.exp(jax.random.uniform(tail_key, (G,), jnp.float32, jnp.log(0.25 * SEQ_LEN), jnp.log(4.0 * SEQ_LEN)))
    head_share = jax.random.uniform(share_key, (G,), jnp.float32, 0.3, 0.7)
    positions = jnp.arange(SEQ_LEN, dtype=jnp.float32)[:, None]
    head_env = jnp.exp(-positions / head_spans[None, :]) * jnp.sqrt(head_share / energy_total(head_spans))[None, :]
    tail_env = jnp.exp(-positions / tail_spans[None, :]) * jnp.sqrt((1.0 - head_share) / energy_total(tail_spans))[None, :]
    rough_taps = jnp.clip(jax.random.normal(tap_key, (SEQ_LEN, G), jnp.float32), -5.0, 5.0)
    return (rough_taps * (head_env + tail_env)).astype(jnp.bfloat16)


def shard_levels(rng, shape, cuts, smallest, top_value):
    gain = 1.0
    for axis_at, parts in cuts:
        steps = jax.random.uniform(jax.random.fold_in(jax.random.fold_in(rng, 6), axis_at), (parts,), jnp.float32, smallest / len(cuts), top_value / len(cuts))
        gain = gain * jnp.repeat(jnp.exp(steps), shape[axis_at] // parts).reshape((-1,) + (1,) * (len(shape) - 1 - axis_at))
    return gain


def normal_values(rng, dims, scale, most, pieces=(), kind=jnp.bfloat16):
    entries = jax.random.normal(rng, dims, jnp.float32) * scale
    if len(pieces) > 0:
        entries = shard_levels(rng, dims, pieces, -0.22, 0.18) * entries
    return jnp.clip(entries, min=-most, max=most).astype(kind)


def setup_inputs(seed: int = 0) -> dict:
    splits = jax.random.split(jax.random.key(seed), 6)
    gate_outer = normal_values(splits[0], (SEQ_LEN, C), 1.0, 6.0, ((0, 16), (1, 2)))
    gate_inner = normal_values(splits[1], (SEQ_LEN, C), 1.0, 6.0, ((0, 16), (1, 2)))
    values_in = normal_values(splits[2], (SEQ_LEN, C), 1.0, 6.0, ((0, 16), (1, 2)))
    filter_taps = draw_filter_taps(jax.random.fold_in(splits[5], 71), 0)
    skip_gain = normal_values(splits[4], (C,), 1.0, 4.0, ((0, 2),), jnp.float32)
    return {"gate_outer": gate_outer, "gate_inner": gate_inner, "values_in": values_in, "filter_taps": filter_taps, "skip_gain": skip_gain}


def reference(gate_outer, gate_inner, values_in, filter_taps, skip_gain):
    mixed_input = (gate_inner.astype(jnp.float32) * values_in.astype(jnp.float32)).astype(jnp.bfloat16)
    signal = mixed_input.astype(jnp.float32)
    fft_size = 2 * SEQ_LEN
    filter_spec = jnp.fft.rfft(filter_taps.astype(jnp.float32), n=fft_size, axis=0)
    blocks = signal.reshape(SEQ_LEN, C // G, G).transpose(1, 0, 2)

    def conv_block(block):
        product = jnp.fft.rfft(block, n=fft_size, axis=0) * filter_spec
        return jnp.fft.irfft(product, n=fft_size, axis=0)[:SEQ_LEN]

    convolved = lax.map(conv_block, blocks).transpose(1, 0, 2).reshape(SEQ_LEN, C)
    gated = gate_outer.astype(jnp.float32) * (convolved + skip_gain[None, :] * signal)
    return gated.astype(jnp.bfloat16)
```

```python
import functools
import math

import jax
import jax.numpy as jnp
from jax import lax
from jax.experimental import pallas as pl
from jax.experimental.pallas import tpu as pltpu
from jax.sharding import PartitionSpec as P

HIGHEST = lax.Precision.HIGHEST


def angle_table(first_index, second_index, modulus):
    product = first_index[:, None] * second_index[None, :] % modulus
    radians = product.astype(jnp.float32) * (2.0 * math.pi / modulus)
    return (jnp.cos(radians), jnp.sin(radians))


def contract(form, table, operand):
    return jnp.einsum(form, table, operand, precision=HIGHEST)


def complex_contract(form, cosine, sine, sign, real_part, imag_part):
    out_real = contract(form, cosine, real_part) - sign * contract(form, sine, imag_part)
    out_imag = contract(form, cosine, imag_part) + sign * contract(form, sine, real_part)
    return (out_real, out_imag)


def rotate(real_part, imag_part, cosine, sine):
    return (real_part * cosine - imag_part * sine, real_part * sine + imag_part * cosine)


def four_step(mixed_input, filter_taps):
    seq_count = lax.axis_size("seq")
    seq_index = lax.axis_index("seq")
    length_dev, width_dev = mixed_input.shape
    class_rows = length_dev // seq_count
    fft_size = 2 * length_dev * seq_count
    filter_local = lax.all_gather(filter_taps, "ch", axis=1, tiled=True)
    got_input, got_filter = (
        lax.all_to_all(mixed_input[None], "seq", split_axis=1, concat_axis=0, tiled=True),
        lax.all_to_all(filter_local[None], "seq", split_axis=1, concat_axis=0, tiled=True),
    )
    got_input = got_input.astype(jnp.float32)
    got_filter = got_filter.astype(jnp.float32)
    source = jnp.arange(seq_count, dtype=jnp.int32)
    pair_second = jnp.where(source == 0, seq_count, 2 * seq_count - source)
    cos_first, sin_first = angle_table(source, source, 2 * seq_count)
    at_zero = seq_index == 0
    cos_second, sin_second = angle_table(pair_second, source, 2 * seq_count)

    def send_parts(received):
        return jnp.stack(
            [
                contract("dp,prc->drc", cos_first, received),
                -contract("dp,prc->drc", sin_first, received),
                contract("dp,prc->drc", cos_second, received),
                -contract("dp,prc->drc", sin_second, received),
            ],
            axis=1,
        )

    sent_input, sent_filter = (
        lax.all_to_all(send_parts(got_input), "seq", split_axis=0, concat_axis=0, tiled=True),
        lax.all_to_all(send_parts(got_filter), "seq", split_axis=0, concat_axis=0, tiled=True),
    )

    def unpack(spectra):
        return (
            jnp.stack([spectra[:, 0], spectra[:, 2]], axis=0),
            jnp.stack([spectra[:, 1], spectra[:, 3]], axis=0),
        )

    my_pair = jnp.stack([seq_index, jnp.where(at_zero, seq_count, 2 * seq_count - seq_index)])
    positions = jnp.arange(length_dev, dtype=jnp.int32)
    cos_twist, sin_twist = angle_table(my_pair, positions, fft_size)
    cos_twist = cos_twist.reshape(2, seq_count, class_rows)
    sin_twist = sin_twist.reshape(2, seq_count, class_rows)
    cos_outer, sin_outer = angle_table(source, source, seq_count)
    inner_index = jnp.arange(class_rows, dtype=jnp.int32)
    cos_mid, sin_mid = angle_table(source, inner_index, length_dev)
    cos_inner, sin_inner = angle_table(inner_index, inner_index, class_rows)

    def finish(spec_real, spec_imag):
        spec_real, spec_imag = rotate(
            spec_real, spec_imag, cos_twist[:, :, :, None], -sin_twist[:, :, :, None]
        )
        spec_real, spec_imag = complex_contract(
            "aq,kqrc->karc", cos_outer, sin_outer, -1.0, spec_real, spec_imag
        )
        spec_real, spec_imag = rotate(
            spec_real, spec_imag, cos_mid[None, :, :, None], -sin_mid[None, :, :, None]
        )
        return complex_contract("br,karc->kabc", cos_inner, sin_inner, -1.0, spec_real, spec_imag)

    input_real, input_imag = finish(*unpack(sent_input))
    filter_real, filter_imag = finish(*unpack(sent_filter))
    repeat = width_dev // filter_real.shape[3]
    filter_real = jnp.tile(filter_real, (1, 1, 1, repeat))
    filter_imag = jnp.tile(filter_imag, (1, 1, 1, repeat))
    prod_real = input_real * filter_real - input_imag * filter_imag
    prod_imag = input_real * filter_imag + input_imag * filter_real
    prod_real, prod_imag = complex_contract(
        "br,kabc->karc", cos_inner, sin_inner, 1.0, prod_real, prod_imag
    )
    prod_real, prod_imag = rotate(
        prod_real, prod_imag, cos_mid[None, :, :, None], sin_mid[None, :, :, None]
    )
    prod_real, prod_imag = complex_contract(
        "aq,karc->kqrc", cos_outer, sin_outer, 1.0, prod_real, prod_imag
    )
    prod_real, prod_imag = rotate(
        prod_real, prod_imag, cos_twist[:, :, :, None], sin_twist[:, :, :, None]
    )
    cos_back, sin_back = angle_table(source, source, 2 * seq_count)
    parts_back = jnp.stack([prod_real[0], prod_imag[0], prod_real[1], prod_imag[1]], axis=1)
    partial_value = lax.all_to_all(parts_back, "seq", split_axis=0, concat_axis=0, tiled=True)
    cos_other, sin_other = angle_table(source, pair_second, 2 * seq_count)
    convolved = (
        contract("pd,drc->prc", cos_back, partial_value[:, 0])
        - contract("pd,drc->prc", sin_back, partial_value[:, 1])
        + contract("pd,drc->prc", cos_other, partial_value[:, 2])
        - contract("pd,drc->prc", sin_other, partial_value[:, 3])
    ) / fft_size
    return lax.all_to_all(convolved, "seq", split_axis=0, concat_axis=1, tiled=True).reshape(
        length_dev, width_dev
    )


def on_device(gate_outer, gate_inner, values_in, filter_taps, skip_gain):
    mixed_input = (gate_inner.astype(jnp.float32) * values_in.astype(jnp.float32)).astype(
        jnp.bfloat16
    )
    convolved = four_step(mixed_input, filter_taps)
    gated = gate_outer.astype(jnp.float32) * (
        convolved + skip_gain[None, :] * mixed_input.astype(jnp.float32)
    )
    return gated.astype(jnp.bfloat16)


LANES = 128
MESH = pl.DeviceIdType.MESH


def conv_kernel(
    seq_count,
    ch_count,
    repeat,
    outer_ref,
    inner_ref,
    values_ref,
    taps_ref,
    skip_ref,
    out_ref,
    mixed_ref,
    taps_send,
    taps_recv,
    taps_wide,
    send_ref,
    recv_ref,
    recv_wide,
    padded_ref,
    toeplitz_ref,
    conv_wide,
    back_send,
    back_recv,
    taps_sems,
    send_sems,
    back_sems,
):
    devices = seq_count * ch_count
    per_dev = taps_send.shape[1]
    members = ch_count * repeat
    pairs = per_dev // 2
    width = out_ref.shape[1]
    seq_at = lax.axis_index("seq")
    ch_at = lax.axis_index("ch")
    me = seq_at * ch_count + ch_at

    def partner(step):
        flat = lax.rem(me + step, devices)
        return lax.div(flat, ch_count), lax.rem(flat, ch_count)

    barrier = pltpu.get_barrier_semaphore()

    @pl.loop(1, devices)
    def _(step):
        to_seq, to_ch = partner(step)
        pl.semaphore_signal(barrier, inc=1, device_id=(to_seq, to_ch), device_id_type=MESH)

    taps_t = taps_ref[...].astype(jnp.float32).T.astype(jnp.bfloat16)
    taps_send[...] = taps_t.reshape(taps_send.shape)

    slots_per_block = LANES // per_dev
    blocks_per_ch = seq_count // slots_per_block

    @pl.loop(0, width // LANES)
    def _(block):
        lanes = pl.ds(pl.multiple_of(block * LANES, LANES), LANES)
        product = inner_ref[:, lanes].astype(jnp.float32) * values_ref[:, lanes].astype(jnp.float32)
        mixed = product.astype(jnp.bfloat16)
        mixed_ref[:, lanes] = mixed
        turned = mixed.astype(jnp.float32).T.astype(jnp.bfloat16)
        rep = block // (ch_count * blocks_per_ch)
        rest = lax.rem(block, ch_count * blocks_per_ch)
        to_ch = rest // blocks_per_ch
        slot = lax.rem(rest, blocks_per_ch) * slots_per_block
        send_ref[rep, to_ch, pl.ds(slot, slots_per_block)] = turned.reshape(
            slots_per_block, per_dev, LANES
        )

    pl.semaphore_wait(barrier, devices - 1)

    own_taps = pltpu.make_async_copy(taps_send.at[seq_at], taps_recv.at[seq_at], taps_sems.at[1])
    own_taps.start()

    @pl.loop(1, seq_count)
    def _(step):
        to_seq = lax.rem(seq_at + step, seq_count)
        pltpu.make_async_remote_copy(
            src_ref=taps_send.at[to_seq],
            dst_ref=taps_recv.at[seq_at],
            send_sem=taps_sems.at[0],
            recv_sem=taps_sems.at[1],
            device_id=(to_seq, ch_at),
            device_id_type=MESH,
        ).start()

    own = pltpu.make_async_copy(send_ref.at[:, ch_at, seq_at], recv_ref.at[me], send_sems.at[1])
    own.start()

    @pl.loop(1, devices)
    def _(step):
        to_seq, to_ch = partner(step)
        pltpu.make_async_remote_copy(
            src_ref=send_ref.at[:, to_ch, to_seq],
            dst_ref=recv_ref.at[me],
            send_sem=send_sems.at[0],
            recv_sem=send_sems.at[1],
            device_id=(to_seq, to_ch),
            device_id_type=MESH,
        ).start()

    pltpu.make_async_copy(taps_recv, taps_recv, taps_sems.at[1]).wait()
    taps_wide[...] = taps_recv[...].reshape(taps_wide.shape).astype(jnp.float32)
    row = lax.broadcasted_iota(jnp.int32, (LANES, LANES), 0)
    col = lax.broadcasted_iota(jnp.int32, (LANES, LANES), 1)
    upper = col >= row

    @pl.loop(0, pairs)
    def _(pair):
        for half in range(2):

            def block_step(lag, before):
                line = taps_wide[pl.ds(lag * per_dev + pair * 2 + half, 1), :]
                spread = jnp.broadcast_to(line, (LANES, LANES))
                rolled = pltpu.roll(spread, 0, 1, stride=1, stride_axis=0)
                toeplitz_ref[
                    pair,
                    pl.ds(pl.multiple_of(lag * LANES, LANES), LANES),
                    half * LANES : (half + 1) * LANES,
                ] = jnp.where(upper, rolled, before).astype(jnp.bfloat16)
                return rolled

            lax.fori_loop(0, seq_count, block_step, jnp.zeros((LANES, LANES), jnp.float32))

    group = 2 * members
    padded_ref[:, 0 : seq_count * group, :] = jnp.zeros(
        (pairs, seq_count * group, LANES), jnp.bfloat16
    )

    pltpu.make_async_copy(recv_ref, recv_ref, send_sems.at[1]).wait()
    block_rows = members * per_dev
    recv_wide[...] = recv_ref[...].reshape(recv_wide.shape).astype(jnp.float32)

    @pl.loop(0, seq_count)
    def _(place):
        for pair in range(pairs):
            first = recv_wide[pl.ds(place * block_rows + 2 * pair, members, stride=per_dev), :]
            second = recv_wide[pl.ds(place * block_rows + 2 * pair + 1, members, stride=per_dev), :]
            padded_ref[pair, pl.ds(pl.multiple_of((seq_count + place) * group, group), group), :] = (
                jnp.concatenate([first, second], axis=0).astype(jnp.bfloat16)
            )

    @pl.loop(0, pairs)
    def _(pair):
        left = jnp.concatenate(
            [
                padded_ref[pair, (seq_count - lag) * group : (2 * seq_count - lag) * group, :]
                for lag in range(seq_count)
            ],
            axis=1,
        )
        total = jnp.dot(left, toeplitz_ref[pair], preferred_element_type=jnp.float32)
        for place in range(seq_count):
            for half in range(2):
                top = place * group + half * members
                conv_wide[
                    pl.ds(place * block_rows + 2 * pair + half, members, stride=per_dev), :
                ] = total[top : top + members, half * LANES : (half + 1) * LANES]

    back_send[...] = conv_wide[...].astype(jnp.bfloat16).reshape(back_send.shape)

    own_back = pltpu.make_async_copy(
        back_send.at[me], back_recv.at[:, ch_at, seq_at], back_sems.at[1]
    )
    own_back.start()

    @pl.loop(1, devices)
    def _(step):
        to_seq, to_ch = partner(step)
        pltpu.make_async_remote_copy(
            src_ref=back_send.at[to_seq * ch_count + to_ch],
            dst_ref=back_recv.at[:, ch_at, seq_at],
            send_sem=back_sems.at[0],
            recv_sem=back_sems.at[1],
            device_id=(to_seq, to_ch),
            device_id_type=MESH,
        ).start()

    pltpu.make_async_copy(back_recv, back_recv, back_sems.at[1]).wait()

    @pl.loop(0, width // LANES)
    def _(block):
        lanes = pl.ds(pl.multiple_of(block * LANES, LANES), LANES)
        rep = block // (ch_count * blocks_per_ch)
        rest = lax.rem(block, ch_count * blocks_per_ch)
        from_ch = rest // blocks_per_ch
        slot = lax.rem(rest, blocks_per_ch) * slots_per_block
        got = back_recv[rep, from_ch, pl.ds(slot, slots_per_block)]
        convolved = got.reshape(LANES, LANES).astype(jnp.float32).T
        mixed = mixed_ref[:, lanes].astype(jnp.float32)
        gated = outer_ref[:, lanes].astype(jnp.float32) * (convolved + skip_ref[:, lanes] * mixed)
        out_ref[:, lanes] = gated.astype(jnp.bfloat16)

    others = pl.ds(0, devices - 1)
    seq_others = pl.ds(0, seq_count - 1)
    pltpu.make_async_copy(
        taps_recv.at[seq_others], taps_recv.at[seq_others], taps_sems.at[0]
    ).wait()
    pltpu.make_async_copy(recv_ref.at[others], recv_ref.at[others], send_sems.at[0]).wait()
    pltpu.make_async_copy(back_send.at[others], back_send.at[others], back_sems.at[0]).wait()


def fused(gate_outer, gate_inner, values_in, filter_taps, skip_gain):
    seq_count = lax.axis_size("seq")
    ch_count = lax.axis_size("ch")
    length_dev, width = gate_outer.shape
    filters = filter_taps.shape[1]
    per_dev = filters // seq_count
    repeat = width // (filters * ch_count)
    devices = seq_count * ch_count
    pairs = per_dev // 2
    members = ch_count * repeat
    length = seq_count * length_dev
    bf16, f32 = jnp.bfloat16, jnp.float32
    return pl.pallas_call(
        functools.partial(conv_kernel, seq_count, ch_count, repeat),
        out_shape=jax.ShapeDtypeStruct((length_dev, width), bf16),
        in_specs=[pl.BlockSpec(memory_space=pltpu.VMEM)] * 5,
        out_specs=pl.BlockSpec(memory_space=pltpu.VMEM),
        scratch_shapes=[
            pltpu.VMEM((length_dev, width), bf16),
            pltpu.VMEM((seq_count, per_dev, LANES), bf16),
            pltpu.VMEM((seq_count, per_dev, LANES), bf16),
            pltpu.VMEM((seq_count * per_dev, LANES), f32),
            pltpu.VMEM((repeat, ch_count, seq_count, per_dev, LANES), bf16),
            pltpu.VMEM((devices, repeat, per_dev, LANES), bf16),
            pltpu.VMEM((width, LANES), f32),
            pltpu.VMEM((pairs, 2 * seq_count * 2 * members, LANES), bf16),
            pltpu.VMEM((pairs, length, 2 * LANES), bf16),
            pltpu.VMEM((width, LANES), f32),
            pltpu.VMEM((devices, repeat, per_dev, LANES), bf16),
            pltpu.VMEM((repeat, ch_count, seq_count, per_dev, LANES), bf16),
            pltpu.SemaphoreType.DMA((2,)),
            pltpu.SemaphoreType.DMA((2,)),
            pltpu.SemaphoreType.DMA((2,)),
        ],
        compiler_params=pltpu.CompilerParams(
            collective_id=0, has_side_effects=True, vmem_limit_bytes=40 * 1024 * 1024
        ),
    )(gate_outer, gate_inner, values_in, filter_taps, skip_gain[None, :])


def whole_filters(gate_outer, filter_taps):
    seq_count = lax.axis_size("seq")
    length_dev, width = gate_outer.shape
    per_dev = filter_taps.shape[1] // seq_count
    members = width // filter_taps.shape[1]
    return length_dev == LANES and per_dev % 16 == 0 and LANES % per_dev == 0 and members == 8


def per_device(gate_outer, gate_inner, values_in, filter_taps, skip_gain):
    run = fused if whole_filters(gate_outer, filter_taps) else on_device
    return run(gate_outer, gate_inner, values_in, filter_taps, skip_gain)


def solution(mesh):
    return jax.shard_map(
        per_device,
        mesh=mesh,
        in_specs=(P("seq", "ch"), P("seq", "ch"), P("seq", "ch"), P("seq", "ch"), P("ch")),
        out_specs=P("seq", "ch"),
        check_vma=False,
    )
```

```python
import functools
import math

import jax
import jax.numpy as jnp
from jax import lax
from jax.experimental import pallas as pl
from jax.experimental.pallas import tpu as pltpu
from jax.sharding import PartitionSpec as P

HIGHEST = lax.Precision.HIGHEST


def angle_table(first_index, second_index, modulus):
    product = first_index[:, None] * second_index[None, :] % modulus
    radians = product.astype(jnp.float32) * (2.0 * math.pi / modulus)
    return (jnp.cos(radians), jnp.sin(radians))


def contract(form, table, operand):
    return jnp.einsum(form, table, operand, precision=HIGHEST)


def complex_contract(form, cosine, sine, sign, real_part, imag_part):
    out_real = contract(form, cosine, real_part) - sign * contract(form, sine, imag_part)
    out_imag = contract(form, cosine, imag_part) + sign * contract(form, sine, real_part)
    return (out_real, out_imag)


def rotate(real_part, imag_part, cosine, sine):
    return (real_part * cosine - imag_part * sine, real_part * sine + imag_part * cosine)


def four_step(mixed_input, filter_taps):
    seq_count = lax.axis_size("seq")
    seq_index = lax.axis_index("seq")
    length_dev, width_dev = mixed_input.shape
    class_rows = length_dev // seq_count
    fft_size = 2 * length_dev * seq_count
    filter_local = lax.all_gather(filter_taps, "ch", axis=1, tiled=True)
    got_input, got_filter = (
        lax.all_to_all(mixed_input[None], "seq", split_axis=1, concat_axis=0, tiled=True),
        lax.all_to_all(filter_local[None], "seq", split_axis=1, concat_axis=0, tiled=True),
    )
    got_input = got_input.astype(jnp.float32)
    got_filter = got_filter.astype(jnp.float32)
    source = jnp.arange(seq_count, dtype=jnp.int32)
    pair_second = jnp.where(source == 0, seq_count, 2 * seq_count - source)
    cos_first, sin_first = angle_table(source, source, 2 * seq_count)
    at_zero = seq_index == 0
    cos_second, sin_second = angle_table(pair_second, source, 2 * seq_count)

    def send_parts(received):
        return jnp.stack(
            [
                contract("dp,prc->drc", cos_first, received),
                -contract("dp,prc->drc", sin_first, received),
                contract("dp,prc->drc", cos_second, received),
                -contract("dp,prc->drc", sin_second, received),
            ],
            axis=1,
        )

    sent_input, sent_filter = (
        lax.all_to_all(send_parts(got_input), "seq", split_axis=0, concat_axis=0, tiled=True),
        lax.all_to_all(send_parts(got_filter), "seq", split_axis=0, concat_axis=0, tiled=True),
    )

    def unpack(spectra):
        return (
            jnp.stack([spectra[:, 0], spectra[:, 2]], axis=0),
            jnp.stack([spectra[:, 1], spectra[:, 3]], axis=0),
        )

    my_pair = jnp.stack([seq_index, jnp.where(at_zero, seq_count, 2 * seq_count - seq_index)])
    positions = jnp.arange(length_dev, dtype=jnp.int32)
    cos_twist, sin_twist = angle_table(my_pair, positions, fft_size)
    cos_twist = cos_twist.reshape(2, seq_count, class_rows)
    sin_twist = sin_twist.reshape(2, seq_count, class_rows)
    cos_outer, sin_outer = angle_table(source, source, seq_count)
    inner_index = jnp.arange(class_rows, dtype=jnp.int32)
    cos_mid, sin_mid = angle_table(source, inner_index, length_dev)
    cos_inner, sin_inner = angle_table(inner_index, inner_index, class_rows)

    def finish(spec_real, spec_imag):
        spec_real, spec_imag = rotate(
            spec_real, spec_imag, cos_twist[:, :, :, None], -sin_twist[:, :, :, None]
        )
        spec_real, spec_imag = complex_contract(
            "aq,kqrc->karc", cos_outer, sin_outer, -1.0, spec_real, spec_imag
        )
        spec_real, spec_imag = rotate(
            spec_real, spec_imag, cos_mid[None, :, :, None], -sin_mid[None, :, :, None]
        )
        return complex_contract("br,karc->kabc", cos_inner, sin_inner, -1.0, spec_real, spec_imag)

    input_real, input_imag = finish(*unpack(sent_input))
    filter_real, filter_imag = finish(*unpack(sent_filter))
    repeat = width_dev // filter_real.shape[3]
    filter_real = jnp.tile(filter_real, (1, 1, 1, repeat))
    filter_imag = jnp.tile(filter_imag, (1, 1, 1, repeat))
    prod_real = input_real * filter_real - input_imag * filter_imag
    prod_imag = input_real * filter_imag + input_imag * filter_real
    prod_real, prod_imag = complex_contract(
        "br,kabc->karc", cos_inner, sin_inner, 1.0, prod_real, prod_imag
    )
    prod_real, prod_imag = rotate(
        prod_real, prod_imag, cos_mid[None, :, :, None], sin_mid[None, :, :, None]
    )
    prod_real, prod_imag = complex_contract(
        "aq,karc->kqrc", cos_outer, sin_outer, 1.0, prod_real, prod_imag
    )
    prod_real, prod_imag = rotate(
        prod_real, prod_imag, cos_twist[:, :, :, None], sin_twist[:, :, :, None]
    )
    cos_back, sin_back = angle_table(source, source, 2 * seq_count)
    parts_back = jnp.stack([prod_real[0], prod_imag[0], prod_real[1], prod_imag[1]], axis=1)
    partial_value = lax.all_to_all(parts_back, "seq", split_axis=0, concat_axis=0, tiled=True)
    cos_other, sin_other = angle_table(source, pair_second, 2 * seq_count)
    convolved = (
        contract("pd,drc->prc", cos_back, partial_value[:, 0])
        - contract("pd,drc->prc", sin_back, partial_value[:, 1])
        + contract("pd,drc->prc", cos_other, partial_value[:, 2])
        - contract("pd,drc->prc", sin_other, partial_value[:, 3])
    ) / fft_size
    return lax.all_to_all(convolved, "seq", split_axis=0, concat_axis=1, tiled=True).reshape(
        length_dev, width_dev
    )


def on_device(gate_outer, gate_inner, values_in, filter_taps, skip_gain):
    mixed_input = (gate_inner.astype(jnp.float32) * values_in.astype(jnp.float32)).astype(
        jnp.bfloat16
    )
    convolved = four_step(mixed_input, filter_taps)
    gated = gate_outer.astype(jnp.float32) * (
        convolved + skip_gain[None, :] * mixed_input.astype(jnp.float32)
    )
    return gated.astype(jnp.bfloat16)


LANES = 128
HALF_ROWS = 8
MESH = pl.DeviceIdType.MESH


def conv_kernel(
    seq_count,
    ch_count,
    repeat,
    outer_hbm,
    inner_hbm,
    values_hbm,
    taps_hbm,
    skip_hbm,
    out_ref,
    outer_ref,
    inner_ref,
    values_ref,
    taps_ref,
    skip_ref,
    mixed_ref,
    taps_send,
    taps_recv,
    taps_wide,
    send_ref,
    recv_ref,
    recv_wide,
    padded_ref,
    toeplitz_ref,
    conv_wide,
    back_send,
    back_recv,
    load_sems,
    taps_sems,
    send_sems,
    back_sems,
):
    devices = seq_count * ch_count
    members = ch_count * repeat
    pairs = HALF_ROWS // 2
    bf16, f32 = jnp.bfloat16, jnp.float32
    seq_at = lax.axis_index("seq")
    ch_at = lax.axis_index("ch")
    me = seq_at * ch_count + ch_at

    loads = [
        pltpu.make_async_copy(source, target, load_sems.at[at])
        for at, (source, target) in enumerate(
            [
                (taps_hbm, taps_ref),
                (inner_hbm, inner_ref),
                (values_hbm, values_ref),
                (outer_hbm, outer_ref),
                (skip_hbm, skip_ref),
            ]
        )
    ]
    for load in loads:
        load.start()

    def partner(step):
        offset = devices // 2 + step // 2 * (2 * (step % 2) - 1)
        flat = lax.rem(me + offset, devices)
        return flat // ch_count, lax.rem(flat, ch_count)

    barrier = pltpu.get_barrier_semaphore()

    @pl.loop(1, devices)
    def _(step):
        to_seq, to_ch = partner(step)
        pl.semaphore_signal(barrier, inc=1, device_id=(to_seq, to_ch), device_id_type=MESH)

    def lanes_of(rep, to_ch, half):
        return pl.ds(((rep * ch_count + to_ch) * 2 + half) * LANES, LANES)

    def interleave(first, second):
        shape = (seq_count, 1, HALF_ROWS, LANES)
        both = jnp.concatenate([first.reshape(shape), second.reshape(shape)], axis=1)
        return both.reshape(seq_count, 2 * HALF_ROWS, LANES).astype(bf16)

    def mix(half):
        for duo in range(repeat // 2):
            for to_ch in range(ch_count):
                turned = []
                for rep in (2 * duo, 2 * duo + 1):
                    lanes = lanes_of(rep, to_ch, half)
                    product = inner_ref[:, lanes].astype(f32) * values_ref[:, lanes].astype(f32)
                    mixed = product.astype(bf16)
                    mixed_ref[:, lanes] = mixed
                    turned.append(mixed.astype(f32).T)
                send_ref[half, duo, to_ch] = interleave(*turned)

    loads[0].wait()
    taps_t = taps_ref[...].astype(f32).T
    taps_send[...] = interleave(taps_t[:LANES], taps_t[LANES:])
    loads[1].wait()
    loads[2].wait()
    mix(0)

    pl.semaphore_wait(barrier, devices - 1)

    pltpu.make_async_copy(taps_send.at[seq_at], taps_recv.at[seq_at], taps_sems.at[1]).start()

    @pl.loop(1, seq_count)
    def _(step):
        to_seq = lax.rem(seq_at + step, seq_count)
        pltpu.make_async_remote_copy(
            src_ref=taps_send.at[to_seq],
            dst_ref=taps_recv.at[seq_at],
            send_sem=taps_sems.at[0],
            recv_sem=taps_sems.at[1],
            device_id=(to_seq, ch_at),
            device_id_type=MESH,
        ).start()

    def send_out(half):
        pltpu.make_async_copy(
            send_ref.at[half, :, ch_at, seq_at], recv_ref.at[half, me], send_sems.at[1, half]
        ).start()

        @pl.loop(1, devices)
        def _(step):
            to_seq, to_ch = partner(step)
            pltpu.make_async_remote_copy(
                src_ref=send_ref.at[half, :, to_ch, to_seq],
                dst_ref=recv_ref.at[half, me],
                send_sem=send_sems.at[0, half],
                recv_sem=send_sems.at[1, half],
                device_id=(to_seq, to_ch),
                device_id_type=MESH,
            ).start()

    send_out(0)
    mix(1)
    send_out(1)

    group = 2 * members
    padded_ref[:, 0 : seq_count * group, :] = jnp.zeros((pairs, seq_count * group, LANES), bf16)

    pltpu.make_async_copy(taps_recv, taps_recv, taps_sems.at[1]).wait()
    taps_wide[...] = taps_recv[...].reshape(taps_wide.shape).astype(f32)
    row = lax.broadcasted_iota(jnp.int32, (LANES, LANES), 0)
    col = lax.broadcasted_iota(jnp.int32, (LANES, LANES), 1)
    upper = col >= row

    @pl.loop(0, 2 * pairs)
    def _(pair):
        for side in range(2):
            before = jnp.zeros((LANES, LANES), f32)
            for lag in range(seq_count):
                line = taps_wide[pl.ds(lag * 2 * HALF_ROWS + pair * 2 + side, 1), :]
                spread = jnp.broadcast_to(line, (LANES, LANES))
                rolled = pltpu.roll(spread, 0, 1, stride=1, stride_axis=0)
                toeplitz_ref[
                    pair, lag * LANES : (lag + 1) * LANES, side * LANES : (side + 1) * LANES
                ] = jnp.where(upper, rolled, before).astype(bf16)
                before = rolled

    block_rows = members * HALF_ROWS

    def convolve(half):
        pltpu.make_async_copy(recv_ref.at[half], recv_ref.at[half], send_sems.at[1, half]).wait()
        recv_wide[...] = recv_ref[half].reshape(recv_wide.shape).astype(f32)

        @pl.loop(0, seq_count)
        def _(place):
            for pair in range(pairs):
                rows = [
                    recv_wide[
                        pl.ds(place * block_rows + 2 * pair + side, members, stride=HALF_ROWS), :
                    ]
                    for side in range(2)
                ]
                padded_ref[
                    pair, pl.ds(pl.multiple_of((seq_count + place) * group, group), group), :
                ] = jnp.concatenate(rows, axis=0).astype(bf16)

        @pl.loop(0, pairs)
        def _(pair):
            left = jnp.concatenate(
                [
                    padded_ref[pair, (seq_count - lag) * group : (2 * seq_count - lag) * group, :]
                    for lag in range(seq_count)
                ],
                axis=1,
            )
            total = jnp.dot(left, toeplitz_ref[half * pairs + pair], preferred_element_type=f32)
            for place in range(seq_count):
                for side in range(2):
                    top = place * group + side * members
                    conv_wide[
                        pl.ds(place * block_rows + 2 * pair + side, members, stride=HALF_ROWS), :
                    ] = total[top : top + members, side * LANES : (side + 1) * LANES]

        back_send[half] = conv_wide[...].astype(bf16).reshape(back_send.shape[1:])
        pltpu.make_async_copy(
            back_send.at[half, me], back_recv.at[half, :, ch_at, seq_at], back_sems.at[1, half]
        ).start()

        @pl.loop(1, devices)
        def _(step):
            to_seq, to_ch = partner(step)
            pltpu.make_async_remote_copy(
                src_ref=back_send.at[half, to_seq * ch_count + to_ch],
                dst_ref=back_recv.at[half, :, ch_at, seq_at],
                send_sem=back_sems.at[0, half],
                recv_sem=back_sems.at[1, half],
                device_id=(to_seq, to_ch),
                device_id_type=MESH,
            ).start()

    convolve(0)
    convolve(1)

    def gate(half):
        pltpu.make_async_copy(back_recv.at[half], back_recv.at[half], back_sems.at[1, half]).wait()
        for duo in range(repeat // 2):
            for from_ch in range(ch_count):
                got = back_recv[half, duo, from_ch].astype(f32)
                got = got.reshape(seq_count, 2, HALF_ROWS, LANES)
                for side in range(2):
                    lanes = lanes_of(2 * duo + side, from_ch, half)
                    convolved = got[:, side].reshape(LANES, LANES).T
                    mixed = mixed_ref[:, lanes].astype(f32)
                    gated = outer_ref[:, lanes].astype(f32) * (
                        convolved + skip_ref[:, lanes] * mixed
                    )
                    out_ref[:, lanes] = gated.astype(bf16)

    loads[3].wait()
    loads[4].wait()
    gate(0)
    gate(1)

    seq_others = taps_recv.at[pl.ds(0, seq_count - 1)]
    pltpu.make_async_copy(seq_others, seq_others, taps_sems.at[0]).wait()
    for half in range(2):
        others = recv_ref.at[half, pl.ds(0, devices - 1)]
        pltpu.make_async_copy(others, others, send_sems.at[0, half]).wait()
        others = back_send.at[half, pl.ds(0, devices - 1)]
        pltpu.make_async_copy(others, others, back_sems.at[0, half]).wait()


def fused(gate_outer, gate_inner, values_in, filter_taps, skip_gain):
    seq_count = lax.axis_size("seq")
    ch_count = lax.axis_size("ch")
    length_dev, width = gate_outer.shape
    filters = filter_taps.shape[1]
    repeat = width // (filters * ch_count)
    devices = seq_count * ch_count
    pairs = HALF_ROWS // 2
    group = 2 * ch_count * repeat
    length = seq_count * length_dev
    tile = 2 * HALF_ROWS
    bf16, f32 = jnp.bfloat16, jnp.float32
    return pl.pallas_call(
        functools.partial(conv_kernel, seq_count, ch_count, repeat),
        out_shape=jax.ShapeDtypeStruct((length_dev, width), bf16),
        in_specs=[pl.BlockSpec(memory_space=pltpu.HBM)] * 5,
        out_specs=pl.BlockSpec(memory_space=pltpu.VMEM),
        scratch_shapes=[
            pltpu.VMEM((length_dev, width), bf16),
            pltpu.VMEM((length_dev, width), bf16),
            pltpu.VMEM((length_dev, width), bf16),
            pltpu.VMEM((length_dev, filters), bf16),
            pltpu.VMEM((1, width), f32),
            pltpu.VMEM((length_dev, width), bf16),
            pltpu.VMEM((seq_count, tile, LANES), bf16),
            pltpu.VMEM((seq_count, tile, LANES), bf16),
            pltpu.VMEM((seq_count * tile, LANES), f32),
            pltpu.VMEM((2, repeat // 2, ch_count, seq_count, tile, LANES), bf16),
            pltpu.VMEM((2, devices, repeat // 2, tile, LANES), bf16),
            pltpu.VMEM((width // 2, LANES), f32),
            pltpu.VMEM((pairs, 2 * seq_count * group, LANES), bf16),
            pltpu.VMEM((2 * pairs, length, 2 * LANES), bf16),
            pltpu.VMEM((width // 2, LANES), f32),
            pltpu.VMEM((2, devices, repeat // 2, tile, LANES), bf16),
            pltpu.VMEM((2, repeat // 2, ch_count, seq_count, tile, LANES), bf16),
            pltpu.SemaphoreType.DMA((5,)),
            pltpu.SemaphoreType.DMA((2,)),
            pltpu.SemaphoreType.DMA((2, 2)),
            pltpu.SemaphoreType.DMA((2, 2)),
        ],
        compiler_params=pltpu.CompilerParams(
            collective_id=0, has_side_effects=True, vmem_limit_bytes=40 * 1024 * 1024
        ),
    )(gate_outer, gate_inner, values_in, filter_taps, skip_gain[None, :])


def whole_filters(gate_outer, filter_taps):
    seq_count = lax.axis_size("seq")
    length_dev, width = gate_outer.shape
    filters = filter_taps.shape[1]
    return (
        length_dev == LANES
        and filters == 2 * LANES
        and seq_count * HALF_ROWS == LANES
        and width == 8 * filters
    )


def per_device(gate_outer, gate_inner, values_in, filter_taps, skip_gain):
    run = fused if whole_filters(gate_outer, filter_taps) else on_device
    return run(gate_outer, gate_inner, values_in, filter_taps, skip_gain)


def solution(mesh):
    return jax.shard_map(
        per_device,
        mesh=mesh,
        in_specs=(P("seq", "ch"), P("seq", "ch"), P("seq", "ch"), P("seq", "ch"), P("ch")),
        out_specs=P("seq", "ch"),
        check_vma=False,
    )
```

```python
import functools
import math

import jax
import jax.numpy as jnp
from jax import lax
from jax.experimental import pallas as pl
from jax.experimental.pallas import tpu as pltpu
from jax.sharding import PartitionSpec as P

HIGHEST = lax.Precision.HIGHEST


def angle_table(first_index, second_index, modulus):
    product = first_index[:, None] * second_index[None, :] % modulus
    radians = product.astype(jnp.float32) * (2.0 * math.pi / modulus)
    return (jnp.cos(radians), jnp.sin(radians))


def contract(form, table, operand):
    return jnp.einsum(form, table, operand, precision=HIGHEST)


def complex_contract(form, cosine, sine, sign, real_part, imag_part):
    out_real = contract(form, cosine, real_part) - sign * contract(form, sine, imag_part)
    out_imag = contract(form, cosine, imag_part) + sign * contract(form, sine, real_part)
    return (out_real, out_imag)


def rotate(real_part, imag_part, cosine, sine):
    return (real_part * cosine - imag_part * sine, real_part * sine + imag_part * cosine)


def four_step(mixed_input, filter_taps):
    seq_count = lax.axis_size("seq")
    seq_index = lax.axis_index("seq")
    length_dev, width_dev = mixed_input.shape
    class_rows = length_dev // seq_count
    fft_size = 2 * length_dev * seq_count
    filter_local = lax.all_gather(filter_taps, "ch", axis=1, tiled=True)
    got_input, got_filter = (
        lax.all_to_all(mixed_input[None], "seq", split_axis=1, concat_axis=0, tiled=True),
        lax.all_to_all(filter_local[None], "seq", split_axis=1, concat_axis=0, tiled=True),
    )
    got_input = got_input.astype(jnp.float32)
    got_filter = got_filter.astype(jnp.float32)
    source = jnp.arange(seq_count, dtype=jnp.int32)
    pair_second = jnp.where(source == 0, seq_count, 2 * seq_count - source)
    cos_first, sin_first = angle_table(source, source, 2 * seq_count)
    at_zero = seq_index == 0
    cos_second, sin_second = angle_table(pair_second, source, 2 * seq_count)

    def send_parts(received):
        return jnp.stack(
            [
                contract("dp,prc->drc", cos_first, received),
                -contract("dp,prc->drc", sin_first, received),
                contract("dp,prc->drc", cos_second, received),
                -contract("dp,prc->drc", sin_second, received),
            ],
            axis=1,
        )

    sent_input, sent_filter = (
        lax.all_to_all(send_parts(got_input), "seq", split_axis=0, concat_axis=0, tiled=True),
        lax.all_to_all(send_parts(got_filter), "seq", split_axis=0, concat_axis=0, tiled=True),
    )

    def unpack(spectra):
        return (
            jnp.stack([spectra[:, 0], spectra[:, 2]], axis=0),
            jnp.stack([spectra[:, 1], spectra[:, 3]], axis=0),
        )

    my_pair = jnp.stack([seq_index, jnp.where(at_zero, seq_count, 2 * seq_count - seq_index)])
    positions = jnp.arange(length_dev, dtype=jnp.int32)
    cos_twist, sin_twist = angle_table(my_pair, positions, fft_size)
    cos_twist = cos_twist.reshape(2, seq_count, class_rows)
    sin_twist = sin_twist.reshape(2, seq_count, class_rows)
    cos_outer, sin_outer = angle_table(source, source, seq_count)
    inner_index = jnp.arange(class_rows, dtype=jnp.int32)
    cos_mid, sin_mid = angle_table(source, inner_index, length_dev)
    cos_inner, sin_inner = angle_table(inner_index, inner_index, class_rows)

    def finish(spec_real, spec_imag):
        spec_real, spec_imag = rotate(
            spec_real, spec_imag, cos_twist[:, :, :, None], -sin_twist[:, :, :, None]
        )
        spec_real, spec_imag = complex_contract(
            "aq,kqrc->karc", cos_outer, sin_outer, -1.0, spec_real, spec_imag
        )
        spec_real, spec_imag = rotate(
            spec_real, spec_imag, cos_mid[None, :, :, None], -sin_mid[None, :, :, None]
        )
        return complex_contract("br,karc->kabc", cos_inner, sin_inner, -1.0, spec_real, spec_imag)

    input_real, input_imag = finish(*unpack(sent_input))
    filter_real, filter_imag = finish(*unpack(sent_filter))
    repeat = width_dev // filter_real.shape[3]
    filter_real = jnp.tile(filter_real, (1, 1, 1, repeat))
    filter_imag = jnp.tile(filter_imag, (1, 1, 1, repeat))
    prod_real = input_real * filter_real - input_imag * filter_imag
    prod_imag = input_real * filter_imag + input_imag * filter_real
    prod_real, prod_imag = complex_contract(
        "br,kabc->karc", cos_inner, sin_inner, 1.0, prod_real, prod_imag
    )
    prod_real, prod_imag = rotate(
        prod_real, prod_imag, cos_mid[None, :, :, None], sin_mid[None, :, :, None]
    )
    prod_real, prod_imag = complex_contract(
        "aq,karc->kqrc", cos_outer, sin_outer, 1.0, prod_real, prod_imag
    )
    prod_real, prod_imag = rotate(
        prod_real, prod_imag, cos_twist[:, :, :, None], sin_twist[:, :, :, None]
    )
    cos_back, sin_back = angle_table(source, source, 2 * seq_count)
    parts_back = jnp.stack([prod_real[0], prod_imag[0], prod_real[1], prod_imag[1]], axis=1)
    partial_value = lax.all_to_all(parts_back, "seq", split_axis=0, concat_axis=0, tiled=True)
    cos_other, sin_other = angle_table(source, pair_second, 2 * seq_count)
    convolved = (
        contract("pd,drc->prc", cos_back, partial_value[:, 0])
        - contract("pd,drc->prc", sin_back, partial_value[:, 1])
        + contract("pd,drc->prc", cos_other, partial_value[:, 2])
        - contract("pd,drc->prc", sin_other, partial_value[:, 3])
    ) / fft_size
    return lax.all_to_all(convolved, "seq", split_axis=0, concat_axis=1, tiled=True).reshape(
        length_dev, width_dev
    )


def on_device(gate_outer, gate_inner, values_in, filter_taps, skip_gain):
    mixed_input = (gate_inner.astype(jnp.float32) * values_in.astype(jnp.float32)).astype(
        jnp.bfloat16
    )
    convolved = four_step(mixed_input, filter_taps)
    gated = gate_outer.astype(jnp.float32) * (
        convolved + skip_gain[None, :] * mixed_input.astype(jnp.float32)
    )
    return gated.astype(jnp.bfloat16)


LANES = 128
HALF_ROWS = 8
MESH = pl.DeviceIdType.MESH


def conv_kernel(
    seq_count,
    ch_count,
    repeat,
    outer_hbm,
    inner_hbm,
    values_hbm,
    taps_hbm,
    skip_hbm,
    out_hbm,
    out_ref,
    outer_ref,
    inner_ref,
    values_ref,
    taps_ref,
    skip_ref,
    mixed_ref,
    taps_send,
    taps_recv,
    taps_wide,
    send_ref,
    recv_ref,
    recv_wide,
    padded_ref,
    toeplitz_ref,
    conv_wide,
    back_send,
    back_recv,
    load_sems,
    taps_sems,
    send_sems,
    back_sems,
    store_sems,
):
    devices = seq_count * ch_count
    members = ch_count * repeat
    pairs = HALF_ROWS // 2
    bf16, f32 = jnp.bfloat16, jnp.float32
    seq_at = lax.axis_index("seq")
    ch_at = lax.axis_index("ch")
    me = seq_at * ch_count + ch_at

    loads = [
        pltpu.make_async_copy(source, target, load_sems.at[at])
        for at, (source, target) in enumerate(
            [
                (taps_hbm, taps_ref),
                (inner_hbm, inner_ref),
                (values_hbm, values_ref),
                (outer_hbm, outer_ref),
                (skip_hbm, skip_ref),
            ]
        )
    ]
    for load in loads:
        load.start()

    def partner(step):
        offset = devices // 2 + step // 2 * (2 * (step % 2) - 1)
        flat = lax.rem(me + offset, devices)
        return flat // ch_count, lax.rem(flat, ch_count)

    barrier = pltpu.get_barrier_semaphore()

    @pl.loop(1, devices)
    def _(step):
        to_seq, to_ch = partner(step)
        pl.semaphore_signal(barrier, inc=1, device_id=(to_seq, to_ch), device_id_type=MESH)

    def lanes_of(rep, to_ch, half):
        return pl.ds(((rep * ch_count + to_ch) * 2 + half) * LANES, LANES)

    def interleave(first, second):
        shape = (seq_count, 1, HALF_ROWS, LANES)
        both = jnp.concatenate([first.reshape(shape), second.reshape(shape)], axis=1)
        return both.reshape(seq_count, 2 * HALF_ROWS, LANES).astype(bf16)

    def mix(half):
        for duo in range(repeat // 2):
            for to_ch in range(ch_count):
                turned = []
                for rep in (2 * duo, 2 * duo + 1):
                    lanes = lanes_of(rep, to_ch, half)
                    product = inner_ref[:, lanes].astype(f32) * values_ref[:, lanes].astype(f32)
                    mixed = product.astype(bf16)
                    mixed_ref[:, lanes] = mixed
                    turned.append(mixed.astype(f32).T)
                send_ref[half, duo, to_ch] = interleave(*turned)

    loads[0].wait()
    taps_t = taps_ref[...].astype(f32).T
    taps_send[...] = interleave(taps_t[:LANES], taps_t[LANES:])
    loads[1].wait()
    loads[2].wait()
    mix(0)

    pl.semaphore_wait(barrier, devices - 1)

    pltpu.make_async_copy(taps_send.at[seq_at], taps_recv.at[seq_at], taps_sems.at[1]).start()

    @pl.loop(1, seq_count)
    def _(step):
        to_seq = lax.rem(seq_at + step, seq_count)
        pltpu.make_async_remote_copy(
            src_ref=taps_send.at[to_seq],
            dst_ref=taps_recv.at[seq_at],
            send_sem=taps_sems.at[0],
            recv_sem=taps_sems.at[1],
            device_id=(to_seq, ch_at),
            device_id_type=MESH,
        ).start()

    def send_out(half):
        pltpu.make_async_copy(
            send_ref.at[half, :, ch_at, seq_at], recv_ref.at[half, me], send_sems.at[1, half]
        ).start()

        @pl.loop(1, devices)
        def _(step):
            to_seq, to_ch = partner(step)
            pltpu.make_async_remote_copy(
                src_ref=send_ref.at[half, :, to_ch, to_seq],
                dst_ref=recv_ref.at[half, me],
                send_sem=send_sems.at[0, half],
                recv_sem=send_sems.at[1, half],
                device_id=(to_seq, to_ch),
                device_id_type=MESH,
            ).start()

    send_out(0)
    mix(1)
    send_out(1)

    group = 2 * members
    padded_ref[:, 0 : seq_count * group, :] = jnp.zeros((pairs, seq_count * group, LANES), bf16)

    pltpu.make_async_copy(taps_recv, taps_recv, taps_sems.at[1]).wait()
    taps_wide[...] = taps_recv[...].reshape(taps_wide.shape).astype(f32)
    row = lax.broadcasted_iota(jnp.int32, (LANES, LANES), 0)
    col = lax.broadcasted_iota(jnp.int32, (LANES, LANES), 1)
    upper = col >= row

    @pl.loop(0, 2 * pairs)
    def _(pair):
        for side in range(2):
            before = jnp.zeros((LANES, LANES), f32)
            for lag in range(seq_count):
                line = taps_wide[pl.ds(lag * 2 * HALF_ROWS + pair * 2 + side, 1), :]
                spread = jnp.broadcast_to(line, (LANES, LANES))
                rolled = pltpu.roll(spread, 0, 1, stride=1, stride_axis=0)
                toeplitz_ref[
                    pair, lag * LANES : (lag + 1) * LANES, side * LANES : (side + 1) * LANES
                ] = jnp.where(upper, rolled, before).astype(bf16)
                before = rolled

    block_rows = members * HALF_ROWS

    def convolve(half):
        pltpu.make_async_copy(recv_ref.at[half], recv_ref.at[half], send_sems.at[1, half]).wait()
        recv_wide[...] = recv_ref[half].reshape(recv_wide.shape).astype(f32)

        @pl.loop(0, seq_count)
        def _(place):
            for pair in range(pairs):
                rows = [
                    recv_wide[
                        pl.ds(place * block_rows + 2 * pair + side, members, stride=HALF_ROWS), :
                    ]
                    for side in range(2)
                ]
                padded_ref[
                    pair, pl.ds(pl.multiple_of((seq_count + place) * group, group), group), :
                ] = jnp.concatenate(rows, axis=0).astype(bf16)

        @pl.loop(0, pairs)
        def _(pair):
            left = jnp.concatenate(
                [
                    padded_ref[pair, (seq_count - lag) * group : (2 * seq_count - lag) * group, :]
                    for lag in range(seq_count)
                ],
                axis=1,
            )
            total = jnp.dot(left, toeplitz_ref[half * pairs + pair], preferred_element_type=f32)
            for place in range(seq_count):
                for side in range(2):
                    top = place * group + side * members
                    conv_wide[
                        pl.ds(place * block_rows + 2 * pair + side, members, stride=HALF_ROWS), :
                    ] = total[top : top + members, side * LANES : (side + 1) * LANES]

        back_send[half] = conv_wide[...].astype(bf16).reshape(back_send.shape[1:])
        pltpu.make_async_copy(
            back_send.at[half, me], back_recv.at[half, :, ch_at, seq_at], back_sems.at[1, half]
        ).start()

        @pl.loop(1, devices)
        def _(step):
            to_seq, to_ch = partner(step)
            pltpu.make_async_remote_copy(
                src_ref=back_send.at[half, to_seq * ch_count + to_ch],
                dst_ref=back_recv.at[half, :, ch_at, seq_at],
                send_sem=back_sems.at[0, half],
                recv_sem=back_sems.at[1, half],
                device_id=(to_seq, to_ch),
                device_id_type=MESH,
            ).start()

    convolve(0)
    convolve(1)

    stores = []

    def gate(half):
        pltpu.make_async_copy(back_recv.at[half], back_recv.at[half], back_sems.at[1, half]).wait()
        for duo in range(repeat // 2):
            for from_ch in range(ch_count):
                got = back_recv[half, duo, from_ch].astype(f32)
                got = got.reshape(seq_count, 2, HALF_ROWS, LANES)
                for side in range(2):
                    lanes = lanes_of(2 * duo + side, from_ch, half)
                    convolved = got[:, side].reshape(LANES, LANES).T
                    mixed = mixed_ref[:, lanes].astype(f32)
                    gated = outer_ref[:, lanes].astype(f32) * (
                        convolved + skip_ref[:, lanes] * mixed
                    )
                    out_ref[:, lanes] = gated.astype(bf16)
                    store = pltpu.make_async_copy(
                        out_ref.at[:, lanes],
                        out_hbm.at[:, lanes],
                        store_sems.at[len(stores)],
                    )
                    store.start()
                    stores.append(store)

    loads[3].wait()
    loads[4].wait()
    gate(0)
    gate(1)

    seq_others = taps_recv.at[pl.ds(0, seq_count - 1)]
    pltpu.make_async_copy(seq_others, seq_others, taps_sems.at[0]).wait()
    for half in range(2):
        others = recv_ref.at[half, pl.ds(0, devices - 1)]
        pltpu.make_async_copy(others, others, send_sems.at[0, half]).wait()
        others = back_send.at[half, pl.ds(0, devices - 1)]
        pltpu.make_async_copy(others, others, back_sems.at[0, half]).wait()
    for store in stores:
        store.wait()


def fused(gate_outer, gate_inner, values_in, filter_taps, skip_gain):
    seq_count = lax.axis_size("seq")
    ch_count = lax.axis_size("ch")
    length_dev, width = gate_outer.shape
    filters = filter_taps.shape[1]
    repeat = width // (filters * ch_count)
    devices = seq_count * ch_count
    pairs = HALF_ROWS // 2
    group = 2 * ch_count * repeat
    length = seq_count * length_dev
    tile = 2 * HALF_ROWS
    bf16, f32 = jnp.bfloat16, jnp.float32
    return pl.pallas_call(
        functools.partial(conv_kernel, seq_count, ch_count, repeat),
        out_shape=jax.ShapeDtypeStruct((length_dev, width), bf16),
        in_specs=[pl.BlockSpec(memory_space=pltpu.HBM)] * 5,
        out_specs=pl.BlockSpec(memory_space=pltpu.HBM),
        scratch_shapes=[
            pltpu.VMEM((length_dev, width), bf16),
            pltpu.VMEM((length_dev, width), bf16),
            pltpu.VMEM((length_dev, width), bf16),
            pltpu.VMEM((length_dev, width), bf16),
            pltpu.VMEM((length_dev, filters), bf16),
            pltpu.VMEM((1, width), f32),
            pltpu.VMEM((length_dev, width), bf16),
            pltpu.VMEM((seq_count, tile, LANES), bf16),
            pltpu.VMEM((seq_count, tile, LANES), bf16),
            pltpu.VMEM((seq_count * tile, LANES), f32),
            pltpu.VMEM((2, repeat // 2, ch_count, seq_count, tile, LANES), bf16),
            pltpu.VMEM((2, devices, repeat // 2, tile, LANES), bf16),
            pltpu.VMEM((width // 2, LANES), f32),
            pltpu.VMEM((pairs, 2 * seq_count * group, LANES), bf16),
            pltpu.VMEM((2 * pairs, length, 2 * LANES), bf16),
            pltpu.VMEM((width // 2, LANES), f32),
            pltpu.VMEM((2, devices, repeat // 2, tile, LANES), bf16),
            pltpu.VMEM((2, repeat // 2, ch_count, seq_count, tile, LANES), bf16),
            pltpu.SemaphoreType.DMA((5,)),
            pltpu.SemaphoreType.DMA((2,)),
            pltpu.SemaphoreType.DMA((2, 2)),
            pltpu.SemaphoreType.DMA((2, 2)),
            pltpu.SemaphoreType.DMA((width // LANES,)),
        ],
        compiler_params=pltpu.CompilerParams(
            collective_id=0, has_side_effects=True, vmem_limit_bytes=64 * 1024 * 1024
        ),
    )(gate_outer, gate_inner, values_in, filter_taps, skip_gain[None, :])


def whole_filters(gate_outer, filter_taps):
    seq_count = lax.axis_size("seq")
    length_dev, width = gate_outer.shape
    filters = filter_taps.shape[1]
    return (
        length_dev == LANES
        and filters == 2 * LANES
        and seq_count * HALF_ROWS == LANES
        and width == 8 * filters
    )


def per_device(gate_outer, gate_inner, values_in, filter_taps, skip_gain):
    run = fused if whole_filters(gate_outer, filter_taps) else on_device
    return run(gate_outer, gate_inner, values_in, filter_taps, skip_gain)


def solution(mesh):
    return jax.shard_map(
        per_device,
        mesh=mesh,
        in_specs=(P("seq", "ch"), P("seq", "ch"), P("seq", "ch"), P("seq", "ch"), P("ch")),
        out_specs=P("seq", "ch"),
        check_vma=False,
    )
```

```python
import functools
import math

import jax
import jax.numpy as jnp
from jax import lax
from jax.experimental import pallas as pl
from jax.experimental.pallas import tpu as pltpu
from jax.sharding import PartitionSpec as P

HIGHEST = lax.Precision.HIGHEST


def angle_table(first_index, second_index, modulus):
    product = first_index[:, None] * second_index[None, :] % modulus
    radians = product.astype(jnp.float32) * (2.0 * math.pi / modulus)
    return (jnp.cos(radians), jnp.sin(radians))


def contract(form, table, operand):
    return jnp.einsum(form, table, operand, precision=HIGHEST)


def complex_contract(form, cosine, sine, sign, real_part, imag_part):
    out_real = contract(form, cosine, real_part) - sign * contract(form, sine, imag_part)
    out_imag = contract(form, cosine, imag_part) + sign * contract(form, sine, real_part)
    return (out_real, out_imag)


def rotate(real_part, imag_part, cosine, sine):
    return (real_part * cosine - imag_part * sine, real_part * sine + imag_part * cosine)


def four_step(mixed_input, filter_taps):
    seq_count = lax.axis_size("seq")
    seq_index = lax.axis_index("seq")
    length_dev, width_dev = mixed_input.shape
    class_rows = length_dev // seq_count
    fft_size = 2 * length_dev * seq_count
    filter_local = lax.all_gather(filter_taps, "ch", axis=1, tiled=True)
    got_input, got_filter = (
        lax.all_to_all(mixed_input[None], "seq", split_axis=1, concat_axis=0, tiled=True),
        lax.all_to_all(filter_local[None], "seq", split_axis=1, concat_axis=0, tiled=True),
    )
    got_input = got_input.astype(jnp.float32)
    got_filter = got_filter.astype(jnp.float32)
    source = jnp.arange(seq_count, dtype=jnp.int32)
    pair_second = jnp.where(source == 0, seq_count, 2 * seq_count - source)
    cos_first, sin_first = angle_table(source, source, 2 * seq_count)
    at_zero = seq_index == 0
    cos_second, sin_second = angle_table(pair_second, source, 2 * seq_count)

    def send_parts(received):
        return jnp.stack(
            [
                contract("dp,prc->drc", cos_first, received),
                -contract("dp,prc->drc", sin_first, received),
                contract("dp,prc->drc", cos_second, received),
                -contract("dp,prc->drc", sin_second, received),
            ],
            axis=1,
        )

    sent_input, sent_filter = (
        lax.all_to_all(send_parts(got_input), "seq", split_axis=0, concat_axis=0, tiled=True),
        lax.all_to_all(send_parts(got_filter), "seq", split_axis=0, concat_axis=0, tiled=True),
    )

    def unpack(spectra):
        return (
            jnp.stack([spectra[:, 0], spectra[:, 2]], axis=0),
            jnp.stack([spectra[:, 1], spectra[:, 3]], axis=0),
        )

    my_pair = jnp.stack([seq_index, jnp.where(at_zero, seq_count, 2 * seq_count - seq_index)])
    positions = jnp.arange(length_dev, dtype=jnp.int32)
    cos_twist, sin_twist = angle_table(my_pair, positions, fft_size)
    cos_twist = cos_twist.reshape(2, seq_count, class_rows)
    sin_twist = sin_twist.reshape(2, seq_count, class_rows)
    cos_outer, sin_outer = angle_table(source, source, seq_count)
    inner_index = jnp.arange(class_rows, dtype=jnp.int32)
    cos_mid, sin_mid = angle_table(source, inner_index, length_dev)
    cos_inner, sin_inner = angle_table(inner_index, inner_index, class_rows)

    def finish(spec_real, spec_imag):
        spec_real, spec_imag = rotate(
            spec_real, spec_imag, cos_twist[:, :, :, None], -sin_twist[:, :, :, None]
        )
        spec_real, spec_imag = complex_contract(
            "aq,kqrc->karc", cos_outer, sin_outer, -1.0, spec_real, spec_imag
        )
        spec_real, spec_imag = rotate(
            spec_real, spec_imag, cos_mid[None, :, :, None], -sin_mid[None, :, :, None]
        )
        return complex_contract("br,karc->kabc", cos_inner, sin_inner, -1.0, spec_real, spec_imag)

    input_real, input_imag = finish(*unpack(sent_input))
    filter_real, filter_imag = finish(*unpack(sent_filter))
    repeat = width_dev // filter_real.shape[3]
    filter_real = jnp.tile(filter_real, (1, 1, 1, repeat))
    filter_imag = jnp.tile(filter_imag, (1, 1, 1, repeat))
    prod_real = input_real * filter_real - input_imag * filter_imag
    prod_imag = input_real * filter_imag + input_imag * filter_real
    prod_real, prod_imag = complex_contract(
        "br,kabc->karc", cos_inner, sin_inner, 1.0, prod_real, prod_imag
    )
    prod_real, prod_imag = rotate(
        prod_real, prod_imag, cos_mid[None, :, :, None], sin_mid[None, :, :, None]
    )
    prod_real, prod_imag = complex_contract(
        "aq,karc->kqrc", cos_outer, sin_outer, 1.0, prod_real, prod_imag
    )
    prod_real, prod_imag = rotate(
        prod_real, prod_imag, cos_twist[:, :, :, None], sin_twist[:, :, :, None]
    )
    cos_back, sin_back = angle_table(source, source, 2 * seq_count)
    parts_back = jnp.stack([prod_real[0], prod_imag[0], prod_real[1], prod_imag[1]], axis=1)
    partial_value = lax.all_to_all(parts_back, "seq", split_axis=0, concat_axis=0, tiled=True)
    cos_other, sin_other = angle_table(source, pair_second, 2 * seq_count)
    convolved = (
        contract("pd,drc->prc", cos_back, partial_value[:, 0])
        - contract("pd,drc->prc", sin_back, partial_value[:, 1])
        + contract("pd,drc->prc", cos_other, partial_value[:, 2])
        - contract("pd,drc->prc", sin_other, partial_value[:, 3])
    ) / fft_size
    return lax.all_to_all(convolved, "seq", split_axis=0, concat_axis=1, tiled=True).reshape(
        length_dev, width_dev
    )


def on_device(gate_outer, gate_inner, values_in, filter_taps, skip_gain):
    mixed_input = (gate_inner.astype(jnp.float32) * values_in.astype(jnp.float32)).astype(
        jnp.bfloat16
    )
    convolved = four_step(mixed_input, filter_taps)
    gated = gate_outer.astype(jnp.float32) * (
        convolved + skip_gain[None, :] * mixed_input.astype(jnp.float32)
    )
    return gated.astype(jnp.bfloat16)


LANES = 128
HALF_ROWS = 8
MESH = pl.DeviceIdType.MESH


def conv_kernel(
    seq_count,
    ch_count,
    repeat,
    outer_hbm,
    inner_hbm,
    values_hbm,
    taps_hbm,
    skip_hbm,
    out_hbm,
    out_ref,
    outer_ref,
    inner_ref,
    values_ref,
    taps_ref,
    skip_ref,
    mixed_ref,
    taps_send,
    taps_recv,
    taps_wide,
    send_ref,
    recv_ref,
    recv_wide,
    padded_ref,
    toeplitz_ref,
    conv_wide,
    back_send,
    back_recv,
    load_sems,
    taps_sems,
    send_sems,
    back_sems,
    store_sems,
):
    devices = seq_count * ch_count
    members = ch_count * repeat
    pairs = HALF_ROWS // 2
    bf16, f32 = jnp.bfloat16, jnp.float32
    seq_at = lax.axis_index("seq")
    ch_at = lax.axis_index("ch")
    me = seq_at * ch_count + ch_at

    loads = [
        pltpu.make_async_copy(source, target, load_sems.at[at])
        for at, (source, target) in enumerate(
            [
                (taps_hbm, taps_ref),
                (inner_hbm, inner_ref),
                (values_hbm, values_ref),
                (outer_hbm, outer_ref),
                (skip_hbm, skip_ref),
            ]
        )
    ]
    for load in loads:
        load.start()

    def partner(step):
        flat = lax.rem(me + step, devices)
        return flat // ch_count, lax.rem(flat, ch_count)

    barrier = pltpu.get_barrier_semaphore()

    @pl.loop(1, devices)
    def _(step):
        to_seq, to_ch = partner(step)
        pl.semaphore_signal(barrier, inc=1, device_id=(to_seq, to_ch), device_id_type=MESH)

    def lanes_of(rep, to_ch, half):
        return pl.ds(((rep * ch_count + to_ch) * 2 + half) * LANES, LANES)

    def interleave(first, second):
        shape = (seq_count, 1, HALF_ROWS, LANES)
        both = jnp.concatenate([first.reshape(shape), second.reshape(shape)], axis=1)
        return both.reshape(seq_count, 2 * HALF_ROWS, LANES).astype(bf16)

    def mix(half):
        for duo in range(repeat // 2):
            for to_ch in range(ch_count):
                turned = []
                for rep in (2 * duo, 2 * duo + 1):
                    lanes = lanes_of(rep, to_ch, half)
                    product = inner_ref[:, lanes].astype(f32) * values_ref[:, lanes].astype(f32)
                    mixed = product.astype(bf16)
                    mixed_ref[:, lanes] = mixed
                    turned.append(mixed.astype(f32).T)
                send_ref[half, duo, to_ch] = interleave(*turned)

    loads[0].wait()
    taps_t = taps_ref[...].astype(f32).T
    taps_send[...] = interleave(taps_t[:LANES], taps_t[LANES:])
    loads[1].wait()
    loads[2].wait()
    mix(0)

    pl.semaphore_wait(barrier, devices - 1)

    pltpu.make_async_copy(taps_send.at[seq_at], taps_recv.at[seq_at], taps_sems.at[1]).start()

    @pl.loop(1, seq_count)
    def _(step):
        to_seq = lax.rem(seq_at + step, seq_count)
        pltpu.make_async_remote_copy(
            src_ref=taps_send.at[to_seq],
            dst_ref=taps_recv.at[seq_at],
            send_sem=taps_sems.at[0],
            recv_sem=taps_sems.at[1],
            device_id=(to_seq, ch_at),
            device_id_type=MESH,
        ).start()

    def send_out(half):
        pltpu.make_async_copy(
            send_ref.at[half, :, ch_at, seq_at], recv_ref.at[half, me], send_sems.at[1, half]
        ).start()

        @pl.loop(1, devices)
        def _(step):
            to_seq, to_ch = partner(step)
            pltpu.make_async_remote_copy(
                src_ref=send_ref.at[half, :, to_ch, to_seq],
                dst_ref=recv_ref.at[half, me],
                send_sem=send_sems.at[0, half],
                recv_sem=send_sems.at[1, half],
                device_id=(to_seq, to_ch),
                device_id_type=MESH,
            ).start()

    send_out(0)
    mix(1)
    send_out(1)

    group = 2 * members
    padded_ref[:, 0 : seq_count * group, :] = jnp.zeros((pairs, seq_count * group, LANES), bf16)

    pltpu.make_async_copy(taps_recv, taps_recv, taps_sems.at[1]).wait()
    taps_wide[...] = taps_recv[...].reshape(taps_wide.shape).astype(f32)
    row = lax.broadcasted_iota(jnp.int32, (LANES, LANES), 0)
    col = lax.broadcasted_iota(jnp.int32, (LANES, LANES), 1)
    upper = col >= row

    @pl.loop(0, 2 * pairs)
    def _(pair):
        for side in range(2):
            before = jnp.zeros((LANES, LANES), f32)
            for lag in range(seq_count):
                line = taps_wide[pl.ds(lag * 2 * HALF_ROWS + pair * 2 + side, 1), :]
                spread = jnp.broadcast_to(line, (LANES, LANES))
                rolled = pltpu.roll(spread, 0, 1, stride=1, stride_axis=0)
                toeplitz_ref[
                    pair, lag * LANES : (lag + 1) * LANES, side * LANES : (side + 1) * LANES
                ] = jnp.where(upper, rolled, before).astype(bf16)
                before = rolled

    block_rows = members * HALF_ROWS

    def convolve(half):
        pltpu.make_async_copy(recv_ref.at[half], recv_ref.at[half], send_sems.at[1, half]).wait()
        recv_wide[...] = recv_ref[half].reshape(recv_wide.shape).astype(f32)

        @pl.loop(0, seq_count)
        def _(place):
            for pair in range(pairs):
                rows = [
                    recv_wide[
                        pl.ds(place * block_rows + 2 * pair + side, members, stride=HALF_ROWS), :
                    ]
                    for side in range(2)
                ]
                padded_ref[
                    pair, pl.ds(pl.multiple_of((seq_count + place) * group, group), group), :
                ] = jnp.concatenate(rows, axis=0).astype(bf16)

        @pl.loop(0, pairs)
        def _(pair):
            left = jnp.concatenate(
                [
                    padded_ref[pair, (seq_count - lag) * group : (2 * seq_count - lag) * group, :]
                    for lag in range(seq_count)
                ],
                axis=1,
            )
            total = jnp.dot(left, toeplitz_ref[half * pairs + pair], preferred_element_type=f32)
            for place in range(seq_count):
                for side in range(2):
                    top = place * group + side * members
                    conv_wide[
                        pl.ds(place * block_rows + 2 * pair + side, members, stride=HALF_ROWS), :
                    ] = total[top : top + members, side * LANES : (side + 1) * LANES]

        back_send[half] = conv_wide[...].astype(bf16).reshape(back_send.shape[1:])
        pltpu.make_async_copy(
            back_send.at[half, me], back_recv.at[half, :, ch_at, seq_at], back_sems.at[1, half]
        ).start()

        @pl.loop(1, devices)
        def _(step):
            to_seq, to_ch = partner(step)
            pltpu.make_async_remote_copy(
                src_ref=back_send.at[half, to_seq * ch_count + to_ch],
                dst_ref=back_recv.at[half, :, ch_at, seq_at],
                send_sem=back_sems.at[0, half],
                recv_sem=back_sems.at[1, half],
                device_id=(to_seq, to_ch),
                device_id_type=MESH,
            ).start()

    convolve(0)
    convolve(1)

    stores = []

    def gate(half):
        pltpu.make_async_copy(back_recv.at[half], back_recv.at[half], back_sems.at[1, half]).wait()
        for duo in range(repeat // 2):
            for from_ch in range(ch_count):
                got = back_recv[half, duo, from_ch].astype(f32)
                got = got.reshape(seq_count, 2, HALF_ROWS, LANES)
                for side in range(2):
                    lanes = lanes_of(2 * duo + side, from_ch, half)
                    convolved = got[:, side].reshape(LANES, LANES).T
                    mixed = mixed_ref[:, lanes].astype(f32)
                    gated = outer_ref[:, lanes].astype(f32) * (
                        convolved + skip_ref[:, lanes] * mixed
                    )
                    out_ref[:, lanes] = gated.astype(bf16)
                    store = pltpu.make_async_copy(
                        out_ref.at[:, lanes],
                        out_hbm.at[:, lanes],
                        store_sems.at[len(stores)],
                    )
                    store.start()
                    stores.append(store)

    loads[3].wait()
    loads[4].wait()
    gate(0)
    gate(1)

    seq_others = taps_recv.at[pl.ds(0, seq_count - 1)]
    pltpu.make_async_copy(seq_others, seq_others, taps_sems.at[0]).wait()
    for half in range(2):
        others = recv_ref.at[half, pl.ds(0, devices - 1)]
        pltpu.make_async_copy(others, others, send_sems.at[0, half]).wait()
        others = back_send.at[half, pl.ds(0, devices - 1)]
        pltpu.make_async_copy(others, others, back_sems.at[0, half]).wait()
    for store in stores:
        store.wait()


def fused(gate_outer, gate_inner, values_in, filter_taps, skip_gain):
    seq_count = lax.axis_size("seq")
    ch_count = lax.axis_size("ch")
    length_dev, width = gate_outer.shape
    filters = filter_taps.shape[1]
    repeat = width // (filters * ch_count)
    devices = seq_count * ch_count
    pairs = HALF_ROWS // 2
    group = 2 * ch_count * repeat
    length = seq_count * length_dev
    tile = 2 * HALF_ROWS
    bf16, f32 = jnp.bfloat16, jnp.float32
    return pl.pallas_call(
        functools.partial(conv_kernel, seq_count, ch_count, repeat),
        out_shape=jax.ShapeDtypeStruct((length_dev, width), bf16),
        in_specs=[pl.BlockSpec(memory_space=pltpu.HBM)] * 5,
        out_specs=pl.BlockSpec(memory_space=pltpu.HBM),
        scratch_shapes=[
            pltpu.VMEM((length_dev, width), bf16),
            pltpu.VMEM((length_dev, width), bf16),
            pltpu.VMEM((length_dev, width), bf16),
            pltpu.VMEM((length_dev, width), bf16),
            pltpu.VMEM((length_dev, filters), bf16),
            pltpu.VMEM((1, width), f32),
            pltpu.VMEM((length_dev, width), bf16),
            pltpu.VMEM((seq_count, tile, LANES), bf16),
            pltpu.VMEM((seq_count, tile, LANES), bf16),
            pltpu.VMEM((seq_count * tile, LANES), f32),
            pltpu.VMEM((2, repeat // 2, ch_count, seq_count, tile, LANES), bf16),
            pltpu.VMEM((2, devices, repeat // 2, tile, LANES), bf16),
            pltpu.VMEM((width // 2, LANES), f32),
            pltpu.VMEM((pairs, 2 * seq_count * group, LANES), bf16),
            pltpu.VMEM((2 * pairs, length, 2 * LANES), bf16),
            pltpu.VMEM((width // 2, LANES), f32),
            pltpu.VMEM((2, devices, repeat // 2, tile, LANES), bf16),
            pltpu.VMEM((2, repeat // 2, ch_count, seq_count, tile, LANES), bf16),
            pltpu.SemaphoreType.DMA((5,)),
            pltpu.SemaphoreType.DMA((2,)),
            pltpu.SemaphoreType.DMA((2, 2)),
            pltpu.SemaphoreType.DMA((2, 2)),
            pltpu.SemaphoreType.DMA((width // LANES,)),
        ],
        compiler_params=pltpu.CompilerParams(
            collective_id=0, has_side_effects=True, vmem_limit_bytes=64 * 1024 * 1024
        ),
    )(gate_outer, gate_inner, values_in, filter_taps, skip_gain[None, :])


def whole_filters(gate_outer, filter_taps):
    seq_count = lax.axis_size("seq")
    length_dev, width = gate_outer.shape
    filters = filter_taps.shape[1]
    return (
        length_dev == LANES
        and filters == 2 * LANES
        and seq_count * HALF_ROWS == LANES
        and width == 8 * filters
    )


def per_device(gate_outer, gate_inner, values_in, filter_taps, skip_gain):
    run = fused if whole_filters(gate_outer, filter_taps) else on_device
    return run(gate_outer, gate_inner, values_in, filter_taps, skip_gain)


def solution(mesh):
    return jax.shard_map(
        per_device,
        mesh=mesh,
        in_specs=(P("seq", "ch"), P("seq", "ch"), P("seq", "ch"), P("seq", "ch"), P("ch")),
        out_specs=P("seq", "ch"),
        check_vma=False,
    )
```

```python
import functools
import math

import jax
import jax.numpy as jnp
from jax import lax
from jax.experimental import pallas as pl
from jax.experimental.pallas import tpu as pltpu
from jax.sharding import PartitionSpec as P

HIGHEST = lax.Precision.HIGHEST


def angle_table(first_index, second_index, modulus):
    product = first_index[:, None] * second_index[None, :] % modulus
    radians = product.astype(jnp.float32) * (2.0 * math.pi / modulus)
    return (jnp.cos(radians), jnp.sin(radians))


def contract(form, table, operand):
    return jnp.einsum(form, table, operand, precision=HIGHEST)


def complex_contract(form, cosine, sine, sign, real_part, imag_part):
    out_real = contract(form, cosine, real_part) - sign * contract(form, sine, imag_part)
    out_imag = contract(form, cosine, imag_part) + sign * contract(form, sine, real_part)
    return (out_real, out_imag)


def rotate(real_part, imag_part, cosine, sine):
    return (real_part * cosine - imag_part * sine, real_part * sine + imag_part * cosine)


def four_step(mixed_input, filter_taps):
    seq_count = lax.axis_size("seq")
    seq_index = lax.axis_index("seq")
    length_dev, width_dev = mixed_input.shape
    class_rows = length_dev // seq_count
    fft_size = 2 * length_dev * seq_count
    filter_local = lax.all_gather(filter_taps, "ch", axis=1, tiled=True)
    got_input, got_filter = (
        lax.all_to_all(mixed_input[None], "seq", split_axis=1, concat_axis=0, tiled=True),
        lax.all_to_all(filter_local[None], "seq", split_axis=1, concat_axis=0, tiled=True),
    )
    got_input = got_input.astype(jnp.float32)
    got_filter = got_filter.astype(jnp.float32)
    source = jnp.arange(seq_count, dtype=jnp.int32)
    pair_second = jnp.where(source == 0, seq_count, 2 * seq_count - source)
    cos_first, sin_first = angle_table(source, source, 2 * seq_count)
    at_zero = seq_index == 0
    cos_second, sin_second = angle_table(pair_second, source, 2 * seq_count)

    def send_parts(received):
        return jnp.stack(
            [
                contract("dp,prc->drc", cos_first, received),
                -contract("dp,prc->drc", sin_first, received),
                contract("dp,prc->drc", cos_second, received),
                -contract("dp,prc->drc", sin_second, received),
            ],
            axis=1,
        )

    sent_input, sent_filter = (
        lax.all_to_all(send_parts(got_input), "seq", split_axis=0, concat_axis=0, tiled=True),
        lax.all_to_all(send_parts(got_filter), "seq", split_axis=0, concat_axis=0, tiled=True),
    )

    def unpack(spectra):
        return (
            jnp.stack([spectra[:, 0], spectra[:, 2]], axis=0),
            jnp.stack([spectra[:, 1], spectra[:, 3]], axis=0),
        )

    my_pair = jnp.stack([seq_index, jnp.where(at_zero, seq_count, 2 * seq_count - seq_index)])
    positions = jnp.arange(length_dev, dtype=jnp.int32)
    cos_twist, sin_twist = angle_table(my_pair, positions, fft_size)
    cos_twist = cos_twist.reshape(2, seq_count, class_rows)
    sin_twist = sin_twist.reshape(2, seq_count, class_rows)
    cos_outer, sin_outer = angle_table(source, source, seq_count)
    inner_index = jnp.arange(class_rows, dtype=jnp.int32)
    cos_mid, sin_mid = angle_table(source, inner_index, length_dev)
    cos_inner, sin_inner = angle_table(inner_index, inner_index, class_rows)

    def finish(spec_real, spec_imag):
        spec_real, spec_imag = rotate(
            spec_real, spec_imag, cos_twist[:, :, :, None], -sin_twist[:, :, :, None]
        )
        spec_real, spec_imag = complex_contract(
            "aq,kqrc->karc", cos_outer, sin_outer, -1.0, spec_real, spec_imag
        )
        spec_real, spec_imag = rotate(
            spec_real, spec_imag, cos_mid[None, :, :, None], -sin_mid[None, :, :, None]
        )
        return complex_contract("br,karc->kabc", cos_inner, sin_inner, -1.0, spec_real, spec_imag)

    input_real, input_imag = finish(*unpack(sent_input))
    filter_real, filter_imag = finish(*unpack(sent_filter))
    repeat = width_dev // filter_real.shape[3]
    filter_real = jnp.tile(filter_real, (1, 1, 1, repeat))
    filter_imag = jnp.tile(filter_imag, (1, 1, 1, repeat))
    prod_real = input_real * filter_real - input_imag * filter_imag
    prod_imag = input_real * filter_imag + input_imag * filter_real
    prod_real, prod_imag = complex_contract(
        "br,kabc->karc", cos_inner, sin_inner, 1.0, prod_real, prod_imag
    )
    prod_real, prod_imag = rotate(
        prod_real, prod_imag, cos_mid[None, :, :, None], sin_mid[None, :, :, None]
    )
    prod_real, prod_imag = complex_contract(
        "aq,karc->kqrc", cos_outer, sin_outer, 1.0, prod_real, prod_imag
    )
    prod_real, prod_imag = rotate(
        prod_real, prod_imag, cos_twist[:, :, :, None], sin_twist[:, :, :, None]
    )
    cos_back, sin_back = angle_table(source, source, 2 * seq_count)
    parts_back = jnp.stack([prod_real[0], prod_imag[0], prod_real[1], prod_imag[1]], axis=1)
    partial_value = lax.all_to_all(parts_back, "seq", split_axis=0, concat_axis=0, tiled=True)
    cos_other, sin_other = angle_table(source, pair_second, 2 * seq_count)
    convolved = (
        contract("pd,drc->prc", cos_back, partial_value[:, 0])
        - contract("pd,drc->prc", sin_back, partial_value[:, 1])
        + contract("pd,drc->prc", cos_other, partial_value[:, 2])
        - contract("pd,drc->prc", sin_other, partial_value[:, 3])
    ) / fft_size
    return lax.all_to_all(convolved, "seq", split_axis=0, concat_axis=1, tiled=True).reshape(
        length_dev, width_dev
    )


def on_device(gate_outer, gate_inner, values_in, filter_taps, skip_gain):
    mixed_input = (gate_inner.astype(jnp.float32) * values_in.astype(jnp.float32)).astype(
        jnp.bfloat16
    )
    convolved = four_step(mixed_input, filter_taps)
    gated = gate_outer.astype(jnp.float32) * (
        convolved + skip_gain[None, :] * mixed_input.astype(jnp.float32)
    )
    return gated.astype(jnp.bfloat16)


LANES = 128
HALF_ROWS = 8
MESH = pl.DeviceIdType.MESH


def conv_kernel(
    seq_count,
    ch_count,
    repeat,
    outer_hbm,
    inner_hbm,
    values_hbm,
    taps_hbm,
    skip_hbm,
    out_hbm,
    out_ref,
    outer_ref,
    inner_ref,
    values_ref,
    taps_ref,
    skip_ref,
    mixed_ref,
    taps_send,
    taps_recv,
    taps_wide,
    send_ref,
    recv_ref,
    recv_wide,
    padded_ref,
    toeplitz_ref,
    conv_wide,
    back_send,
    back_recv,
    load_sems,
    taps_sems,
    send_sems,
    back_sems,
    store_sems,
):
    devices = seq_count * ch_count
    members = ch_count * repeat
    pairs = HALF_ROWS // 2
    bf16, f32 = jnp.bfloat16, jnp.float32
    seq_at = lax.axis_index("seq")
    ch_at = lax.axis_index("ch")
    me = seq_at * ch_count + ch_at

    loads = [
        pltpu.make_async_copy(source, target, load_sems.at[at])
        for at, (source, target) in enumerate(
            [
                (taps_hbm, taps_ref),
                (inner_hbm, inner_ref),
                (values_hbm, values_ref),
                (outer_hbm, outer_ref),
                (skip_hbm, skip_ref),
            ]
        )
    ]
    for load in loads:
        load.start()

    def partner(step):
        flat = lax.rem(me + step, devices)
        return flat // ch_count, lax.rem(flat, ch_count)

    barrier = pltpu.get_barrier_semaphore()

    @pl.loop(1, devices)
    def _(step):
        to_seq, to_ch = partner(step)
        pl.semaphore_signal(barrier, inc=1, device_id=(to_seq, to_ch), device_id_type=MESH)

    def lanes_of(rep, to_ch, half):
        return pl.ds(((rep * ch_count + to_ch) * 2 + half) * LANES, LANES)

    def interleave(first, second):
        shape = (seq_count, 1, HALF_ROWS, LANES)
        both = jnp.concatenate([first.reshape(shape), second.reshape(shape)], axis=1)
        return both.reshape(seq_count, 2 * HALF_ROWS, LANES).astype(bf16)

    def mix(half):
        for duo in range(repeat // 2):
            for to_ch in range(ch_count):
                turned = []
                for rep in (2 * duo, 2 * duo + 1):
                    lanes = lanes_of(rep, to_ch, half)
                    product = inner_ref[:, lanes].astype(f32) * values_ref[:, lanes].astype(f32)
                    mixed = product.astype(bf16)
                    mixed_ref[:, lanes] = mixed
                    turned.append(mixed.astype(f32).T)
                send_ref[half, duo, to_ch] = interleave(*turned)

    loads[0].wait()
    taps_t = taps_ref[...].astype(f32).T
    taps_send[...] = interleave(taps_t[:LANES], taps_t[LANES:])
    loads[1].wait()
    loads[2].wait()
    mix(0)
    mix(1)

    pl.semaphore_wait(barrier, devices - 1)

    pltpu.make_async_copy(taps_send.at[seq_at], taps_recv.at[seq_at], taps_sems.at[1]).start()

    @pl.loop(1, seq_count)
    def _(step):
        to_seq = lax.rem(seq_at + step, seq_count)
        pltpu.make_async_remote_copy(
            src_ref=taps_send.at[to_seq],
            dst_ref=taps_recv.at[seq_at],
            send_sem=taps_sems.at[0],
            recv_sem=taps_sems.at[1],
            device_id=(to_seq, ch_at),
            device_id_type=MESH,
        ).start()

    def send_out(half):
        pltpu.make_async_copy(
            send_ref.at[half, :, ch_at, seq_at], recv_ref.at[half, me], send_sems.at[1, half]
        ).start()

        @pl.loop(1, devices)
        def _(step):
            to_seq, to_ch = partner(step)
            pltpu.make_async_remote_copy(
                src_ref=send_ref.at[half, :, to_ch, to_seq],
                dst_ref=recv_ref.at[half, me],
                send_sem=send_sems.at[0, half],
                recv_sem=send_sems.at[1, half],
                device_id=(to_seq, to_ch),
                device_id_type=MESH,
            ).start()

    send_out(0)
    send_out(1)

    group = 2 * members
    padded_ref[:, 0 : seq_count * group, :] = jnp.zeros((pairs, seq_count * group, LANES), bf16)

    pltpu.make_async_copy(taps_recv, taps_recv, taps_sems.at[1]).wait()
    taps_wide[...] = taps_recv[...].reshape(taps_wide.shape).astype(f32)
    row = lax.broadcasted_iota(jnp.int32, (LANES, LANES), 0)
    col = lax.broadcasted_iota(jnp.int32, (LANES, LANES), 1)
    upper = col >= row

    block_rows = members * HALF_ROWS

    def convolve(half):
        @pl.loop(half * pairs, (half + 1) * pairs)
        def _(pair):
            for side in range(2):
                before = jnp.zeros((LANES, LANES), f32)
                for lag in range(seq_count):
                    line = taps_wide[pl.ds(lag * 2 * HALF_ROWS + pair * 2 + side, 1), :]
                    spread = jnp.broadcast_to(line, (LANES, LANES))
                    rolled = pltpu.roll(spread, 0, 1, stride=1, stride_axis=0)
                    toeplitz_ref[
                        pair, lag * LANES : (lag + 1) * LANES, side * LANES : (side + 1) * LANES
                    ] = jnp.where(upper, rolled, before).astype(bf16)
                    before = rolled

        pltpu.make_async_copy(recv_ref.at[half], recv_ref.at[half], send_sems.at[1, half]).wait()
        recv_wide[...] = recv_ref[half].reshape(recv_wide.shape).astype(f32)

        @pl.loop(0, seq_count)
        def _(place):
            for pair in range(pairs):
                rows = [
                    recv_wide[
                        pl.ds(place * block_rows + 2 * pair + side, members, stride=HALF_ROWS), :
                    ]
                    for side in range(2)
                ]
                padded_ref[
                    pair, pl.ds(pl.multiple_of((seq_count + place) * group, group), group), :
                ] = jnp.concatenate(rows, axis=0).astype(bf16)

        @pl.loop(0, pairs)
        def _(pair):
            left = jnp.concatenate(
                [
                    padded_ref[pair, (seq_count - lag) * group : (2 * seq_count - lag) * group, :]
                    for lag in range(seq_count)
                ],
                axis=1,
            )
            total = jnp.dot(left, toeplitz_ref[half * pairs + pair], preferred_element_type=f32)
            for place in range(seq_count):
                for side in range(2):
                    top = place * group + side * members
                    conv_wide[
                        pl.ds(place * block_rows + 2 * pair + side, members, stride=HALF_ROWS), :
                    ] = total[top : top + members, side * LANES : (side + 1) * LANES]

        back_send[half] = conv_wide[...].astype(bf16).reshape(back_send.shape[1:])
        pltpu.make_async_copy(
            back_send.at[half, me], back_recv.at[half, :, ch_at, seq_at], back_sems.at[1, half]
        ).start()

        @pl.loop(1, devices)
        def _(step):
            to_seq, to_ch = partner(step)
            pltpu.make_async_remote_copy(
                src_ref=back_send.at[half, to_seq * ch_count + to_ch],
                dst_ref=back_recv.at[half, :, ch_at, seq_at],
                send_sem=back_sems.at[0, half],
                recv_sem=back_sems.at[1, half],
                device_id=(to_seq, to_ch),
                device_id_type=MESH,
            ).start()

    convolve(0)
    convolve(1)

    stores = []

    def gate(half):
        pltpu.make_async_copy(back_recv.at[half], back_recv.at[half], back_sems.at[1, half]).wait()
        for duo in range(repeat // 2):
            for from_ch in range(ch_count):
                got = back_recv[half, duo, from_ch].astype(f32)
                got = got.reshape(seq_count, 2, HALF_ROWS, LANES)
                for side in range(2):
                    lanes = lanes_of(2 * duo + side, from_ch, half)
                    convolved = got[:, side].reshape(LANES, LANES).T
                    mixed = mixed_ref[:, lanes].astype(f32)
                    gated = outer_ref[:, lanes].astype(f32) * (
                        convolved + skip_ref[:, lanes] * mixed
                    )
                    out_ref[:, lanes] = gated.astype(bf16)
                    store = pltpu.make_async_copy(
                        out_ref.at[:, lanes],
                        out_hbm.at[:, lanes],
                        store_sems.at[len(stores)],
                    )
                    store.start()
                    stores.append(store)

    loads[3].wait()
    loads[4].wait()
    gate(0)
    gate(1)

    seq_others = taps_recv.at[pl.ds(0, seq_count - 1)]
    pltpu.make_async_copy(seq_others, seq_others, taps_sems.at[0]).wait()
    for half in range(2):
        others = recv_ref.at[half, pl.ds(0, devices - 1)]
        pltpu.make_async_copy(others, others, send_sems.at[0, half]).wait()
        others = back_send.at[half, pl.ds(0, devices - 1)]
        pltpu.make_async_copy(others, others, back_sems.at[0, half]).wait()
    for store in stores:
        store.wait()


def fused(gate_outer, gate_inner, values_in, filter_taps, skip_gain):
    seq_count = lax.axis_size("seq")
    ch_count = lax.axis_size("ch")
    length_dev, width = gate_outer.shape
    filters = filter_taps.shape[1]
    repeat = width // (filters * ch_count)
    devices = seq_count * ch_count
    pairs = HALF_ROWS // 2
    group = 2 * ch_count * repeat
    length = seq_count * length_dev
    tile = 2 * HALF_ROWS
    bf16, f32 = jnp.bfloat16, jnp.float32
    return pl.pallas_call(
        functools.partial(conv_kernel, seq_count, ch_count, repeat),
        out_shape=jax.ShapeDtypeStruct((length_dev, width), bf16),
        in_specs=[pl.BlockSpec(memory_space=pltpu.HBM)] * 5,
        out_specs=pl.BlockSpec(memory_space=pltpu.HBM),
        scratch_shapes=[
            pltpu.VMEM((length_dev, width), bf16),
            pltpu.VMEM((length_dev, width), bf16),
            pltpu.VMEM((length_dev, width), bf16),
            pltpu.VMEM((length_dev, width), bf16),
            pltpu.VMEM((length_dev, filters), bf16),
            pltpu.VMEM((1, width), f32),
            pltpu.VMEM((length_dev, width), bf16),
            pltpu.VMEM((seq_count, tile, LANES), bf16),
            pltpu.VMEM((seq_count, tile, LANES), bf16),
            pltpu.VMEM((seq_count * tile, LANES), f32),
            pltpu.VMEM((2, repeat // 2, ch_count, seq_count, tile, LANES), bf16),
            pltpu.VMEM((2, devices, repeat // 2, tile, LANES), bf16),
            pltpu.VMEM((width // 2, LANES), f32),
            pltpu.VMEM((pairs, 2 * seq_count * group, LANES), bf16),
            pltpu.VMEM((2 * pairs, length, 2 * LANES), bf16),
            pltpu.VMEM((width // 2, LANES), f32),
            pltpu.VMEM((2, devices, repeat // 2, tile, LANES), bf16),
            pltpu.VMEM((2, repeat // 2, ch_count, seq_count, tile, LANES), bf16),
            pltpu.SemaphoreType.DMA((5,)),
            pltpu.SemaphoreType.DMA((2,)),
            pltpu.SemaphoreType.DMA((2, 2)),
            pltpu.SemaphoreType.DMA((2, 2)),
            pltpu.SemaphoreType.DMA((width // LANES,)),
        ],
        compiler_params=pltpu.CompilerParams(
            collective_id=0, has_side_effects=True, vmem_limit_bytes=64 * 1024 * 1024
        ),
    )(gate_outer, gate_inner, values_in, filter_taps, skip_gain[None, :])


def whole_filters(gate_outer, filter_taps):
    seq_count = lax.axis_size("seq")
    length_dev, width = gate_outer.shape
    filters = filter_taps.shape[1]
    return (
        length_dev == LANES
        and filters == 2 * LANES
        and seq_count * HALF_ROWS == LANES
        and width == 8 * filters
    )


def per_device(gate_outer, gate_inner, values_in, filter_taps, skip_gain):
    run = fused if whole_filters(gate_outer, filter_taps) else on_device
    return run(gate_outer, gate_inner, values_in, filter_taps, skip_gain)


def solution(mesh):
    return jax.shard_map(
        per_device,
        mesh=mesh,
        in_specs=(P("seq", "ch"), P("seq", "ch"), P("seq", "ch"), P("seq", "ch"), P("ch")),
        out_specs=P("seq", "ch"),
        check_vma=False,
    )
```
